1024 devices in a mesh: dp: 32 (over z), expert: 4 (over x_lo, core), tensor: 8 (over y, x_hi).
Axes of the slice: x: 4 (x_hi: 2, x_lo: 2; x = x_hi * 2 + x_lo), y: 4, z: 32, core: 2. Of those that a mesh axis runs over, the one named last changes fastest.
Arguments:
- tokens: bfloat16 [256, 6144], P('dp'), may hold values from -6 to 6
- expert_ids: int32 [256, 2], P('dp'), may hold values from 0 to 3, all different within a row; in each aligned block of 8 rows (0 to 7, 8 to 15, ...) at most 5 rows name the same one
- gates: float32 [256, 2], P('dp'), may hold values from 0.1 to 1
- w_gate: bfloat16 [4, 8192, 6144], P('expert', 'tensor', 'dp'), may hold values from -0.078125 to 0.078125
- w_up: bfloat16 [4, 8192, 6144], P('expert', 'tensor', 'dp'), may hold values from -0.078125 to 0.078125
- w_out: bfloat16 [4, 8192, 6144], P('expert', 'tensor', 'dp'), may hold values from -0.0625 to 0.0625
- cotangent: bfloat16 [256, 6144], P('dp'), may hold values from -6 to 6
Outputs:
- mixed: bfloat16 [256, 6144], P('dp', ('expert', 'tensor'))
- d_tokens: bfloat16 [256, 6144], P('dp', ('expert', 'tensor'))
- d_gate: bfloat16 [4, 8192, 6144], P('expert', 'tensor', 'dp')
- d_up: bfloat16 [4, 8192, 6144], P('expert', 'tensor', 'dp')
- d_out: bfloat16 [4, 8192, 6144], P('expert', 'tensor', 'dp')
The draws below stay inside these ranges and needn't reach their ends.
Inputs may be any that keep to these rules, and one draw needn't show every extreme that they name: `expert_ids`: each token names two different experts. Among the 8 tokens of one dp index no expert is named more than 5 times, a bound that some block reaches.
All inputs are finite; a program needn't handle non-finite values.
Results may differ from the reference program's by a relative error of at most 0.0057.
Values may be sent and summed in bfloat16 or wider, within the bound.
A program may use at most 32 MiB of HBM per device.

```python
import math
import jax
import jax.numpy as jnp
import numpy as np
from jax import lax

D = 6144
FF = 8192
CAP = 5
EXPERTS = 4
TOK_DP = 8
TOKENS = 256
N_DP = 32


def shard_levels(stream_key, dims, cuts, smallest, largest):
    loudness, own = 1.0, jax.random.fold_in(stream_key, 6)
    for position, shards_of in cuts:
        draws = jnp.exp(jax.random.uniform(jax.random.fold_in(own, position), (shards_of,), jnp.float32, smallest / len(cuts), largest / len(cuts)))
        loudness = loudness * jnp.repeat(draws, dims[position] // shards_of).reshape([-1 if axis == position else 1 for axis in range(len(dims))])
    return loudness


def routed_block(own_key, own, number, rows, count, top, bound, skew):
    ranking = jax.random.permutation(own_key, count)
    heavy_load, common = shares(count, rows * top, bound, skew, True), shares(count, rows * top, bound, skew, False)
    places = jnp.arange(count)

    def named(tallies, offset_by):
        used = int((tallies > 0).sum())
        fixed = max(1, used // 4)
        moved = fixed + (places - fixed + offset_by * (used - fixed)) % max(1, count - fixed)
        return jnp.zeros((count,), jnp.int32).at[ranking[jnp.where(places < fixed, places, moved)]].set(jnp.asarray(tallies, jnp.int32))

    tallies = jnp.where(number % 4 == 0, named(heavy_load, number // 4), named(common, number - number // 4 - 1))
    mixed = jax.random.permutation(jax.random.fold_in(own, 3), count)
    source_of, sink = mixed[0:count // 2 * 2:2], mixed[1:count // 2 * 2:2]
    margin = jnp.minimum(tallies[source_of] - 1, bound - tallies[sink]) // 2
    margin = jnp.where((source_of == ranking[0]) | (sink == ranking[0]) | (tallies[sink] == 0), 0, jnp.maximum(margin, 0))
    moved = jax.random.randint(jax.random.fold_in(own, 4), (count // 2,), 0, 1 << 20) % (margin + 1)
    tallies = tallies.at[source_of].add(-moved).at[sink].add(moved)
    labels = jnp.searchsorted(jnp.cumsum(tallies), jnp.arange(rows * top), side="right").astype(jnp.int32)
    grid = labels.reshape(top, rows).T
    grid = grid[jax.random.permutation(jax.random.fold_in(own, 1), rows)]
    offset_by = jax.random.randint(jax.random.fold_in(own, 2), (rows, 1), 0, top)
    return jnp.take_along_axis(grid, (jnp.arange(top)[None, :] + offset_by) % top, axis=1)


def shares(amount, total, most, slope, full):
    portions = [(1 << 20) // math.isqrt(rank ** slope) + 1 for rank in range(1, amount + 1)]
    largest = most if full else min(most, max(-(-total // amount), total * portions[0] // sum(portions)))
    least = 1 if total - largest >= amount - 1 else 0
    holding, spare = [largest] + [least] * (amount - 1), total - largest - least * (amount - 1)
    while spare > 0:
        movable = [i for i in range(1, amount) if holding[i] < largest] or [i for i in range(1, amount) if holding[i] < most]
        mass, remaining = sum([portions[i] for i in movable]), spare
        for i in movable:
            extra = min(most - holding[i], max(1, remaining * portions[i] // mass), spare)
            holding[i] = holding[i] + extra
            spare = spare - extra
    return np.array(holding)


def noise(own_key, shape, width, bound, cuts=(), held_as=jnp.bfloat16):
    values = width * jax.random.normal(own_key, shape, jnp.float32)
    if cuts:
        values = values * shard_levels(own_key, shape, cuts, -0.22, 0.18)
    return jnp.clip(values, -bound, bound).astype(held_as)


def setup_inputs(seed: int = 0) -> dict:
    keys = jax.random.split(jax.random.key(seed), 8)
    tokens = noise(keys[0], (TOKENS, D), 1.0, 6.0, ((0, 32),))
    expert_ids_keys = jax.random.split(jax.random.fold_in(keys[1], 1), TOKENS // TOK_DP)
    expert_ids_turns = jax.random.permutation(jax.random.fold_in(keys[1], 3), TOKENS // TOK_DP)
    expert_ids = jax.vmap(lambda own, number: routed_block(jax.random.fold_in(keys[1], 2), own, number, TOK_DP, EXPERTS, 2, CAP, 1))(expert_ids_keys, expert_ids_turns).reshape((TOKENS, 2))
    gates = jnp.clip(0.1 + 0.9 * jax.random.uniform(keys[2], (TOKENS, 2), jnp.float32) ** shard_levels(keys[2], (TOKENS, 2), ((0, 32),), -0.2, 0.2), 0.1, 1.0)
    w_gate = noise(keys[3], (EXPERTS, FF, D), D ** -0.5, 0.078125, ((0, 4), (1, 8), (2, 32)))
    w_up = noise(keys[4], (EXPERTS, FF, D), D ** -0.5, 0.078125, ((0, 4), (1, 8), (2, 32)))
    w_out = noise(keys[5], (EXPERTS, FF, D), FF ** -0.5, 0.0625, ((0, 4), (1, 8), (2, 32)))
    cotangent = noise(keys[6], (TOKENS, D), 1.0, 6.0, ((0, 32),))
    return {"tokens": tokens, "expert_ids": expert_ids, "gates": gates, "w_gate": w_gate, "w_up": w_up, "w_out": w_out, "cotangent": cotangent}


def slot_table(expert_ids):
    groups = expert_ids.reshape(N_DP, TOK_DP * 2)
    onehot = (groups[:, :, None] == jnp.arange(EXPERTS, dtype=jnp.int32)[None, None, :]).astype(jnp.int32)
    earlier = jnp.cumsum(onehot, axis=1) - onehot
    return jnp.sum(earlier * onehot, axis=2).astype(jnp.int32)


def reference(tokens, expert_ids, gates, w_gate, w_up, w_out, cotangent):
    highest = lax.Precision.HIGHEST
    slots = slot_table(expert_ids)
    groups = expert_ids.reshape(N_DP, TOK_DP * 2)
    gate_flat = gates.reshape(N_DP, TOK_DP * 2)
    x_groups = tokens.astype(jnp.float32).reshape(N_DP, TOK_DP, D)
    dy_groups = cotangent.astype(jnp.float32).reshape(N_DP, TOK_DP, D)
    cap_ids = jnp.arange(CAP, dtype=jnp.int32)

    def one_expert(carry, index):
        mixed_acc, grad_acc = carry
        chosen = groups == index
        hits = (chosen[:, None, :] & (slots[:, None, :] == cap_ids[None, :, None])).astype(jnp.float32)
        picks = hits.reshape(N_DP, CAP, TOK_DP, 2).sum(axis=3)
        weighted = (hits * gate_flat[:, None, :]).reshape(N_DP, CAP, TOK_DP, 2).sum(axis=3)
        rows = jnp.einsum('dct,dtf->dcf', picks, x_groups, precision=highest).astype(jnp.bfloat16).reshape(N_DP * CAP, D)
        cot_rows = jnp.einsum('dct,dtf->dcf', weighted, dy_groups, precision=highest).astype(jnp.bfloat16).reshape(N_DP * CAP, D)
        wg = lax.dynamic_index_in_dim(w_gate, index, 0, keepdims=False)
        wu = lax.dynamic_index_in_dim(w_up, index, 0, keepdims=False)
        wo = lax.dynamic_index_in_dim(w_out, index, 0, keepdims=False)
        gate_act = jnp.dot(rows, wg.T, preferred_element_type=jnp.float32)
        up_act = jnp.dot(rows, wu.T, preferred_element_type=jnp.float32)
        active = jax.nn.silu(gate_act)
        hidden = (active * up_act).astype(jnp.bfloat16)
        expert_out = jnp.dot(hidden, wo, preferred_element_type=jnp.float32)
        d_hidden = jnp.dot(cot_rows, wo.T, preferred_element_type=jnp.float32)
        d_out = jnp.dot(hidden.T, cot_rows, preferred_element_type=jnp.float32).astype(jnp.bfloat16)
        sig = jax.nn.sigmoid(gate_act)
        grad_gate = (d_hidden * up_act * (sig * (1.0 + gate_act * (1.0 - sig)))).astype(jnp.bfloat16)
        grad_up = (d_hidden * active).astype(jnp.bfloat16)
        d_gate = jnp.dot(grad_gate.T, rows, preferred_element_type=jnp.float32).astype(jnp.bfloat16)
        d_up = jnp.dot(grad_up.T, rows, preferred_element_type=jnp.float32).astype(jnp.bfloat16)
        row_grad = jnp.dot(grad_gate, wg, preferred_element_type=jnp.float32) + jnp.dot(grad_up, wu, preferred_element_type=jnp.float32)
        mixed_acc = mixed_acc + jnp.einsum('dct,dcf->dtf', weighted, expert_out.reshape(N_DP, CAP, D), precision=highest)
        grad_acc = grad_acc + jnp.einsum('dct,dcf->dtf', picks, row_grad.reshape(N_DP, CAP, D), precision=highest)
        return (mixed_acc, grad_acc), (d_gate, d_up, d_out)

    start = (jnp.zeros((N_DP, TOK_DP, D), jnp.float32), jnp.zeros((N_DP, TOK_DP, D), jnp.float32))
    (mixed_acc, grad_acc), (d_gate, d_up, d_out) = lax.scan(one_expert, start, jnp.arange(EXPERTS, dtype=jnp.int32))
    mixed = mixed_acc.reshape(TOKENS, D).astype(jnp.bfloat16)
    d_tokens = grad_acc.reshape(TOKENS, D).astype(jnp.bfloat16)
    return (mixed, d_tokens, d_gate, d_up, d_out)
```

```python
import functools

import jax
import jax.numpy as jnp
from jax import lax
from jax.experimental import pallas as pl
from jax.experimental.pallas import tpu as pltpu
from jax.sharding import PartitionSpec as P

MESH = pl.DeviceIdType.MESH
F32 = jnp.float32
BF16 = jnp.bfloat16
LANES = 128
EMPTY = -1024.0


def iota(shape, axis):
    return lax.broadcasted_iota(jnp.int32, shape, axis)


def nn(a, b):
    return jnp.dot(a, b, preferred_element_type=F32)


def nt(a, b):
    return lax.dot_general(a, b, (((1,), (1,)), ((), ())), preferred_element_type=F32)


def tn(a, b):
    return lax.dot_general(a, b, (((0,), (0,)), ((), ())), preferred_element_type=F32)


def split3(v):
    hi = v.astype(BF16).astype(F32)
    mid = (v - hi).astype(BF16).astype(F32)
    return hi, mid, v - hi - mid


def source_block(index, feats, tok_ref, cot_ref, ids_ref, gates_ref):
    group = tok_ref.shape[0]
    wide = 2 * feats

    def features(ref):
        start = pl.multiple_of((index // 2) * wide, LANES)
        pair = ref[:, pl.ds(start, wide)].astype(F32)
        turned = pltpu.roll(pair, feats, 1)
        odd = lax.rem(jnp.full((group, wide), index, jnp.int32), 2) == 1
        return jnp.where(odd, turned, pair)[:, :256]

    eye = iota((group, group), 0) == iota((group, group), 1)
    before = iota((group, group), 1) < iota((group, group), 0)

    def column(row):
        spread = jnp.broadcast_to(row, (group, group))
        return jnp.sum(jnp.where(eye, spread, 0.0), axis=1, keepdims=True)

    ids = ids_ref[...].astype(F32)
    id_rows = [ids[k : k + 1, :] for k in range(2)]
    id_cols = [column(row) for row in id_rows]
    gate_cols = [column(gates_ref[k : k + 1, :]) for k in range(2)]

    def slots(k):
        own = jnp.broadcast_to(id_cols[k], (group, group))
        same = [
            (own == jnp.broadcast_to(row, (group, group))).astype(F32) for row in id_rows
        ]
        return jnp.sum(jnp.where(before, same[0] + same[1], 0.0), axis=1, keepdims=True)

    lane = iota((group, 256), 1)

    def per_expert(offset, values, other):
        at = (lane - offset).astype(F32)
        return jnp.where(
            at == id_cols[0], values[0], jnp.where(at == id_cols[1], values[1], other)
        )

    parts = [split3(column) for column in gate_cols]
    meta = per_expert(feats, [slots(0), slots(1)], EMPTY)
    for n in range(3):
        gate = per_expert(feats + 8 * (n + 1), [parts[0][n], parts[1][n]], 0.0)
        meta = jnp.where(lane >= feats + 8 * (n + 1), gate, meta)

    def joined(ref):
        return jnp.where(lane < feats, features(ref), meta)

    return jnp.concatenate([joined(tok_ref), joined(cot_ref)], axis=0).astype(BF16)


def kernel(
    sizes,
    tok_ref, ids_ref, gates_ref, wg_ref, wu_ref, wo_ref, cot_ref,
    mixed_ref, dtok_ref, dg_ref, du_ref, do_ref,
    blk, gathered, select, gate_mat, rows_buf, part, from_left, from_right,
    acts, wide_acts, terms, outgo, income, last, final,
    swap_sem, plane_send, plane_recv, right_send, right_recv, left_send, left_recv,
    ag_right_send, ag_right_recv, ag_left_send, ag_left_recv,
    back_send, back_recv, end_sem,
):
    n, tensor, capacity = sizes
    feats, hidden_units = wg_ref.shape
    group = tok_ref.shape[0]
    rows_n = capacity * n
    hops_right = n // 2
    hops_left = n - 1 - hops_right
    lane_blocks = hidden_units // LANES
    chunk = part.shape[2]

    z = lax.axis_index("dp")
    e = lax.axis_index("expert")
    t = lax.axis_index("tensor")
    index = e * tensor + t
    right = (lax.rem(z + 1, n), e, t)
    left = (lax.rem(z + n - 1, n), e, t)
    partner = (index, z // tensor, lax.rem(z, tensor))
    away = z != index

    def peer(j):
        return (z, j // tensor, lax.rem(j, tensor))

    barrier = pltpu.get_barrier_semaphore()

    def greet(k, _):
        j = lax.rem(index + k, n)
        pl.semaphore_signal(barrier, inc=1, device_id=peer(j), device_id_type=MESH)
        return 0

    lax.fori_loop(1, n, greet, 0)
    for neighbour in (left, right):
        pl.semaphore_signal(barrier, inc=1, device_id=neighbour, device_id_type=MESH)

    @pl.when(away)
    def _():
        pl.semaphore_signal(barrier, inc=1, device_id=partner, device_id_type=MESH)

    blk[...] = source_block(index, feats, tok_ref, cot_ref, ids_ref, gates_ref)
    pl.semaphore_wait(barrier, n + 1 + jnp.where(away, 1, 0))

    def swap():
        return pltpu.make_async_remote_copy(
            src_ref=blk, dst_ref=gathered.at[z], send_sem=swap_sem.at[0],
            recv_sem=swap_sem.at[1], device_id=partner, device_id_type=MESH,
        )

    @pl.when(away)
    def _():
        swap().start()
        swap().wait()

    @pl.when(jnp.logical_not(away))
    def _():
        gathered[index] = blk[...]

    def spread(k):
        j = lax.rem(index + k, n)
        return pltpu.make_async_remote_copy(
            src_ref=gathered.at[index], dst_ref=gathered.at[index],
            send_sem=plane_send.at[k], recv_sem=plane_recv.at[index],
            device_id=peer(j), device_id_type=MESH,
        )

    def arrival(k):
        j = lax.rem(index + n - k, n)
        return pltpu.make_async_remote_copy(
            src_ref=gathered.at[j], dst_ref=gathered.at[j],
            send_sem=plane_send.at[k], recv_sem=plane_recv.at[j],
            device_id=peer(j), device_id_type=MESH,
        )

    lax.fori_loop(1, n, lambda k, _: (spread(k).start(), 0)[1], 0)
    lax.fori_loop(1, n, lambda k, _: (arrival(k).wait_recv(), 0)[1], 0)

    lines = n * 2 * group
    block = gathered[...].reshape(lines, 256)
    meta = block[:, LANES:]
    base = feats - LANES
    pick = (iota((LANES, 2 * rows_n), 0) == base + e).astype(F32).astype(BF16)
    slot = nn(meta, pick)
    line = iota((lines, 2 * rows_n), 0)
    inner = lax.rem(line, 2 * group)
    place = capacity * (line // (2 * group)) + jnp.where(inner < group, 0, rows_n)
    sel = (slot + place.astype(F32) == iota((lines, 2 * rows_n), 1).astype(F32)).astype(F32)
    sel = sel.astype(BF16)
    select[...] = sel
    depth = iota((LANES, feats), 0) - base - e
    gate_pick = ((depth == 8) | (depth == 16) | (depth == 24)).astype(F32).astype(BF16)
    gate = nn(meta, gate_pick)
    gate_mat[...] = gate
    is_token = lax.rem(iota((lines, feats), 0), 2 * group) < group
    scaled = (block[:, :feats].astype(F32) * jnp.where(is_token, 1.0, gate)).astype(BF16)
    rows_all = tn(sel, scaled).astype(BF16)
    rows_buf[...] = rows_all
    rows = rows_all[:rows_n]
    cot_rows = rows_all[rows_n:]

    for a, (left_arg, w_ref) in enumerate(
        ((rows, wg_ref), (rows, wu_ref), (cot_rows, wo_ref))
    ):
        product = nn(left_arg, w_ref[...])
        for r in range(rows_n // chunk):
            for c in range(lane_blocks):
                part[r * lane_blocks + c, a] = product[
                    r * chunk : (r + 1) * chunk, c * LANES : (c + 1) * LANES
                ]

    def to_right(s, a, src):
        return pltpu.make_async_remote_copy(
            src_ref=src, dst_ref=from_left.at[s, a], send_sem=right_send.at[s, a],
            recv_sem=right_recv.at[s, a], device_id=right, device_id_type=MESH,
        )

    def to_left(s, a, src):
        return pltpu.make_async_remote_copy(
            src_ref=src, dst_ref=from_right.at[s, a], send_sem=left_send.at[s, a],
            recv_sem=left_recv.at[s, a], device_id=left, device_id_type=MESH,
        )

    def right_chunk(s):
        return lax.rem(z + hops_right - s + n, n)

    def left_chunk(s):
        return lax.rem(z - hops_left + s + n, n)

    def right_step(s, a):
        held = from_left.at[s - 1, a]
        to_right(s - 1, a, held).wait_recv()
        held[...] += part[right_chunk(s), a]
        to_right(s, a, held).start()

    def left_step(s, a):
        held = from_right.at[s - 1, a]
        to_left(s - 1, a, held).wait_recv()
        held[...] += part[left_chunk(s), a]
        to_left(s, a, held).start()

    for a in range(3):
        to_right(0, a, part.at[right_chunk(0), a]).start()
        to_left(0, a, part.at[left_chunk(0), a]).start()

    def both(s, _):
        for a in range(3):
            right_step(s, a)
            left_step(s, a)
        return 0

    lax.fori_loop(1, hops_left, both, 0)
    for s in range(hops_left, hops_right):
        for a in range(3):
            right_step(s, a)
    sums = []
    for a in range(3):
        to_right(hops_right - 1, a, from_left.at[hops_right - 1, a]).wait_recv()
        to_left(hops_left - 1, a, from_right.at[hops_left - 1, a]).wait_recv()
        sums.append(
            from_left[hops_right - 1, a] + from_right[hops_left - 1, a] + part[z, a]
        )

    gate_act, up_act, d_hidden = sums
    sig = jax.nn.sigmoid(gate_act)
    active = gate_act * sig
    grad_gate = d_hidden * up_act * (sig * (1.0 + gate_act * (1.0 - sig)))
    grad_up = d_hidden * active
    pad = acts.shape[1] - 3 * chunk
    acts[z] = jnp.concatenate(
        [active * up_act, grad_gate, grad_up, jnp.zeros((pad, LANES), F32)], axis=0
    ).astype(BF16)

    def ag_right(s, owner):
        return pltpu.make_async_remote_copy(
            src_ref=acts.at[owner], dst_ref=acts.at[owner], send_sem=ag_right_send.at[s],
            recv_sem=ag_right_recv.at[s], device_id=right, device_id_type=MESH,
        )

    def ag_left(s, owner):
        return pltpu.make_async_remote_copy(
            src_ref=acts.at[owner], dst_ref=acts.at[owner], send_sem=ag_left_send.at[s],
            recv_sem=ag_left_recv.at[s], device_id=left, device_id_type=MESH,
        )

    def unpack(owner):
        piece = acts[owner].astype(F32)
        row = pl.multiple_of((owner // lane_blocks) * chunk, 8)
        col = pl.multiple_of(lax.rem(owner, lane_blocks) * LANES, LANES)
        for a in range(3):
            wide_acts[a, pl.ds(row, chunk), pl.ds(col, LANES)] = piece[
                a * chunk : (a + 1) * chunk
            ]

    def owner_right(s):
        return lax.rem(z - s + n, n)

    def owner_left(s):
        return lax.rem(z + s, n)

    ag_right(0, z).start()
    ag_left(0, z).start()
    unpack(z)

    def ag_both(s, _):
        ag_right(s - 1, owner_right(s)).wait_recv()
        ag_right(s, owner_right(s)).start()
        ag_left(s - 1, owner_left(s)).wait_recv()
        ag_left(s, owner_left(s)).start()
        unpack(owner_right(s))
        unpack(owner_left(s))
        return 0

    lax.fori_loop(1, hops_left, ag_both, 0)
    for s in range(hops_left, hops_right):
        ag_right(s - 1, owner_right(s)).wait_recv()
        ag_right(s, owner_right(s)).start()
        unpack(owner_right(s))
    ag_left(hops_left - 1, owner_left(hops_left)).wait_recv()
    unpack(owner_left(hops_left))
    ag_right(hops_right - 1, owner_right(hops_right)).wait_recv()
    unpack(owner_right(hops_right))

    hidden_all = wide_acts[0].astype(BF16)
    gg_all = wide_acts[1].astype(BF16)
    gu_all = wide_acts[2].astype(BF16)

    terms[:rows_n] = nt(hidden_all, wo_ref[...])
    terms[rows_n:] = nt(gg_all, wg_ref[...]) + nt(gu_all, wu_ref[...])
    whole = terms[...]
    high = whole.astype(BF16)
    low = (whole - high.astype(F32)).astype(BF16)
    table = select[...]
    per_token = nn(table, high) + nn(table, low)
    per_token = per_token * jnp.where(is_token, gate_mat[...], 1.0)
    outgo[...] = per_token.reshape(n, 2 * group, feats)

    def send_back(k):
        j = lax.rem(index + k, n)
        return pltpu.make_async_remote_copy(
            src_ref=outgo.at[j], dst_ref=income.at[index],
            send_sem=back_send.at[k], recv_sem=back_recv.at[index],
            device_id=peer(j), device_id_type=MESH,
        )

    def got_back(k):
        j = lax.rem(index + n - k, n)
        return pltpu.make_async_remote_copy(
            src_ref=outgo.at[j], dst_ref=income.at[j],
            send_sem=back_send.at[k], recv_sem=back_recv.at[j],
            device_id=peer(j), device_id_type=MESH,
        )

    lax.fori_loop(1, n, lambda k, _: (send_back(k).start(), 0)[1], 0)
    income[index] = outgo[index]

    rows_kept = rows_buf[:rows_n]
    do_ref[...] = tn(rows_buf[rows_n:], hidden_all).astype(BF16)
    dg_ref[...] = tn(rows_kept, gg_all).astype(BF16)
    du_ref[...] = tn(rows_kept, gu_all).astype(BF16)

    lax.fori_loop(1, n, lambda k, _: (got_back(k).wait_recv(), 0)[1], 0)
    last[...] = jnp.sum(income[...], axis=0).astype(BF16)

    def finish():
        return pltpu.make_async_remote_copy(
            src_ref=last, dst_ref=final, send_sem=end_sem.at[0],
            recv_sem=end_sem.at[1], device_id=partner, device_id_type=MESH,
        )

    @pl.when(away)
    def _():
        finish().start()

    @pl.when(jnp.logical_not(away))
    def _():
        final[...] = last[...]

    def sent_plane(k, _):
        spread(k).wait_send()
        send_back(k).wait_send()
        return 0

    lax.fori_loop(1, n, sent_plane, 0)

    def sent_right(s, _):
        for a in range(3):
            to_right(s, a, from_left.at[s, a]).wait_send()
        ag_right(s, z).wait_send()
        return 0

    lax.fori_loop(0, hops_right, sent_right, 0)

    def sent_left(s, _):
        for a in range(3):
            to_left(s, a, from_right.at[s, a]).wait_send()
        ag_left(s, z).wait_send()
        return 0

    lax.fori_loop(0, hops_left, sent_left, 0)

    @pl.when(away)
    def _():
        finish().wait()

    done = final[...].astype(F32)
    mixed_ref[...] = done[:group].astype(BF16)
    dtok_ref[...] = done[group:].astype(BF16)


def per_device(n, tensor, experts, tokens, expert_ids, gates, w_gate, w_up, w_out, cotangent):
    group, model = tokens.shape
    _, hidden_units, feats = w_gate.shape
    capacity = 2 * (group // experts) + 1
    rows_n = capacity * n
    chunk = rows_n * (hidden_units // LANES) // n
    hops_right = n // 2
    hops_left = n - 1 - hops_right
    packed = -(-3 * chunk // 16) * 16
    vmem = pl.BlockSpec(memory_space=pltpu.VMEM)
    dma = pltpu.SemaphoreType.DMA
    weight = jax.ShapeDtypeStruct((feats, hidden_units), BF16)
    small = jax.ShapeDtypeStruct((group, feats), BF16)
    mixed, d_tokens, d_gate, d_up, d_out = pl.pallas_call(
        functools.partial(kernel, (n, tensor, capacity)),
        out_shape=(small, small, weight, weight, weight),
        in_specs=[vmem] * 7,
        out_specs=(vmem,) * 5,
        scratch_shapes=[
            pltpu.VMEM((2 * group, 256), BF16),
            pltpu.VMEM((n, 2 * group, 256), BF16),
            pltpu.VMEM((n * 2 * group, 2 * rows_n), BF16),
            pltpu.VMEM((n * 2 * group, feats), F32),
            pltpu.VMEM((2 * rows_n, feats), BF16),
            pltpu.VMEM((n, 3, chunk, LANES), F32),
            pltpu.VMEM((hops_right, 3, chunk, LANES), F32),
            pltpu.VMEM((hops_left, 3, chunk, LANES), F32),
            pltpu.VMEM((n, packed, LANES), BF16),
            pltpu.VMEM((3, rows_n, hidden_units), F32),
            pltpu.VMEM((2 * rows_n, feats), F32),
            pltpu.VMEM((n, 2 * group, feats), F32),
            pltpu.VMEM((n, 2 * group, feats), F32),
            pltpu.VMEM((2 * group, feats), BF16),
            pltpu.VMEM((2 * group, feats), BF16),
            dma((2,)),
            dma((n,)),
            dma((n,)),
            dma((hops_right, 3)),
            dma((hops_right, 3)),
            dma((hops_left, 3)),
            dma((hops_left, 3)),
            dma((hops_right,)),
            dma((hops_right,)),
            dma((hops_left,)),
            dma((hops_left,)),
            dma((n,)),
            dma((n,)),
            dma((2,)),
        ],
        compiler_params=pltpu.CompilerParams(
            collective_id=0, has_side_effects=True, vmem_limit_bytes=40 * 1024 * 1024
        ),
    )(
        tokens, expert_ids.T, gates.T, w_gate[0].T, w_up[0].T, w_out[0].T, cotangent
    )
    return (mixed, d_tokens, d_gate.T[None], d_up.T[None], d_out.T[None])


def solution(mesh):
    sizes = (mesh.shape["dp"], mesh.shape["tensor"], mesh.shape["expert"])
    return jax.shard_map(
        functools.partial(per_device, *sizes),
        mesh=mesh,
        in_specs=(
            P("dp", None),
            P("dp", None),
            P("dp", None),
            P("expert", "tensor", "dp"),
            P("expert", "tensor", "dp"),
            P("expert", "tensor", "dp"),
            P("dp", None),
        ),
        out_specs=(
            P("dp", ("expert", "tensor")),
            P("dp", ("expert", "tensor")),
            P("expert", "tensor", "dp"),
            P("expert", "tensor", "dp"),
            P("expert", "tensor", "dp"),
        ),
        check_vma=False,
    )
```

```python
import functools

import jax
import jax.numpy as jnp
from jax import lax
from jax.experimental import pallas as pl
from jax.experimental.pallas import tpu as pltpu
from jax.sharding import PartitionSpec as P

MESH = pl.DeviceIdType.MESH
F32 = jnp.float32
BF16 = jnp.bfloat16
LANES = 128
EMPTY = -1024.0
STRIDE = 4
PIECES = 2
NEIGHBOURS = (1, -1, 2, -2, STRIDE, -STRIDE)
HALF_RIGHT = 2
HALF_LEFT = 1


def iota(shape, axis):
    return lax.broadcasted_iota(jnp.int32, shape, axis)


def nn(a, b):
    return jnp.dot(a, b, preferred_element_type=F32)


def nt(a, b):
    return lax.dot_general(a, b, (((1,), (1,)), ((), ())), preferred_element_type=F32)


def tn(a, b):
    return lax.dot_general(a, b, (((0,), (0,)), ((), ())), preferred_element_type=F32)


def split3(v):
    hi = v.astype(BF16).astype(F32)
    mid = (v - hi).astype(BF16).astype(F32)
    return hi, mid, v - hi - mid


def source_block(index, feats, tok_ref, cot_ref, ids_ref, gates_ref):
    group = tok_ref.shape[0]
    wide = 2 * feats

    def features(ref):
        start = pl.multiple_of((index // 2) * wide, LANES)
        pair = ref[:, pl.ds(start, wide)].astype(F32)
        turned = pltpu.roll(pair, feats, 1)
        odd = lax.rem(jnp.full((group, wide), index, jnp.int32), 2) == 1
        return jnp.where(odd, turned, pair)[:, :256]

    eye = iota((group, group), 0) == iota((group, group), 1)
    before = iota((group, group), 1) < iota((group, group), 0)

    def column(row):
        spread = jnp.broadcast_to(row, (group, group))
        return jnp.sum(jnp.where(eye, spread, 0.0), axis=1, keepdims=True)

    ids = ids_ref[...].astype(F32)
    id_rows = [ids[k : k + 1, :] for k in range(2)]
    id_cols = [column(row) for row in id_rows]
    gate_cols = [column(gates_ref[k : k + 1, :]) for k in range(2)]

    def slots(k):
        own = jnp.broadcast_to(id_cols[k], (group, group))
        same = [
            (own == jnp.broadcast_to(row, (group, group))).astype(F32) for row in id_rows
        ]
        return jnp.sum(jnp.where(before, same[0] + same[1], 0.0), axis=1, keepdims=True)

    lane = iota((group, 256), 1)

    def per_expert(offset, values, other):
        at = (lane - offset).astype(F32)
        return jnp.where(
            at == id_cols[0], values[0], jnp.where(at == id_cols[1], values[1], other)
        )

    parts = [split3(column) for column in gate_cols]
    meta = per_expert(feats, [slots(0), slots(1)], EMPTY)
    for n in range(3):
        gate = per_expert(feats + 8 * (n + 1), [parts[0][n], parts[1][n]], 0.0)
        meta = jnp.where(lane >= feats + 8 * (n + 1), gate, meta)

    def joined(ref):
        return jnp.where(lane < feats, features(ref), meta)

    return jnp.concatenate([joined(tok_ref), joined(cot_ref)], axis=0).astype(BF16)


def kernel(
    sizes,
    tok_hbm, ids_hbm, gates_hbm, wg_hbm, wu_hbm, wo_hbm, cot_hbm,
    mixed_ref, dtok_ref, dg_ref, du_ref, do_ref,
    tok_ref, ids_ref, gates_ref, wg_ref, wu_ref, wo_ref, cot_ref, load_sem,
    blk, gathered, select, gate_mat, rows_buf, part, packed, near, half_out, half_in, full_out, full_in,
    acts, wide_acts, terms, outgo, income, last, final,
    swap_sem, plane_send, plane_recv, near_send, near_recv, chain_send, chain_recv,
    ag_send, ag_recv, share_send, share_recv, back_send, back_recv, end_sem,
):
    n, tensor, capacity = sizes
    feats, hidden_units = wg_hbm.shape
    group = tok_ref.shape[0]
    rows_n = capacity * n
    leaders = n // STRIDE
    hops_right = leaders // 2
    hops_left = leaders - 1 - hops_right
    lane_blocks = hidden_units // LANES
    chunk = rows_n * lane_blocks // n
    used, full = 3 * chunk, part.shape[1]
    piece = full // PIECES

    loads = [
        pltpu.make_async_copy(src, dst, load_sem.at[k])
        for k, (src, dst) in enumerate((
            (tok_hbm, tok_ref), (cot_hbm, cot_ref), (ids_hbm, ids_ref), (gates_hbm, gates_ref),
            (wg_hbm, wg_ref), (wu_hbm, wu_ref), (wo_hbm, wo_ref),
        ))
    ]
    for load in loads:
        load.start()

    z = lax.axis_index("dp")
    e = lax.axis_index("expert")
    t = lax.axis_index("tensor")
    index = e * tensor + t

    def along(step):
        return (lax.rem(z + step + n, n), e, t)

    partner = (index, z // tensor, lax.rem(z, tensor))
    away = z != index

    def peer(j):
        return (z, j // tensor, lax.rem(j, tensor))

    barrier = pltpu.get_barrier_semaphore()

    @pl.when(away)
    def _():
        pl.semaphore_signal(barrier, inc=1, device_id=partner, device_id_type=MESH)

    for step in NEIGHBOURS:
        pl.semaphore_signal(barrier, inc=1, device_id=along(step), device_id_type=MESH)

    def greet(k, _):
        j = lax.rem(index + k, n)
        pl.semaphore_signal(barrier, inc=1, device_id=peer(j), device_id_type=MESH)
        return 0

    lax.fori_loop(1, n, greet, 0)
    for load in loads[:4]:
        load.wait()
    blk[...] = source_block(index, feats, tok_ref, cot_ref, ids_ref, gates_ref)
    pl.semaphore_wait(barrier, n - 1 + len(NEIGHBOURS) + jnp.where(away, 1, 0))

    def swap():
        return pltpu.make_async_remote_copy(
            src_ref=blk, dst_ref=gathered.at[z], send_sem=swap_sem.at[0],
            recv_sem=swap_sem.at[1], device_id=partner, device_id_type=MESH,
        )

    @pl.when(away)
    def _():
        swap().start()
        swap().wait()

    @pl.when(jnp.logical_not(away))
    def _():
        gathered[index] = blk[...]

    def spread(k):
        j = lax.rem(index + k, n)
        return pltpu.make_async_remote_copy(
            src_ref=gathered.at[index], dst_ref=gathered.at[index],
            send_sem=plane_send.at[k], recv_sem=plane_recv.at[index],
            device_id=peer(j), device_id_type=MESH,
        )

    def arrival(k):
        j = lax.rem(index + n - k, n)
        return pltpu.make_async_remote_copy(
            src_ref=gathered.at[j], dst_ref=gathered.at[j],
            send_sem=plane_send.at[k], recv_sem=plane_recv.at[j],
            device_id=peer(j), device_id_type=MESH,
        )

    lax.fori_loop(1, n, lambda k, _: (spread(k).start(), 0)[1], 0)
    lax.fori_loop(1, n, lambda k, _: (arrival(k).wait_recv(), 0)[1], 0)

    lines = n * 2 * group
    block = gathered[...].reshape(lines, 256)
    meta = block[:, LANES:]
    base = feats - LANES
    pick = (iota((LANES, 2 * rows_n), 0) == base + e).astype(F32).astype(BF16)
    slot = nn(meta, pick)
    line = iota((lines, 2 * rows_n), 0)
    inner = lax.rem(line, 2 * group)
    place = capacity * (line // (2 * group)) + jnp.where(inner < group, 0, rows_n)
    sel = (slot + place.astype(F32) == iota((lines, 2 * rows_n), 1).astype(F32)).astype(F32)
    sel = sel.astype(BF16)
    select[...] = sel
    depth = iota((LANES, feats), 0) - base - e
    gate_pick = ((depth == 8) | (depth == 16) | (depth == 24)).astype(F32).astype(BF16)
    gate = nn(meta, gate_pick)
    gate_mat[...] = gate
    is_token = lax.rem(iota((lines, feats), 0), 2 * group) < group
    scaled = (block[:, :feats].astype(F32) * jnp.where(is_token, 1.0, gate)).astype(BF16)
    rows_all = tn(sel, scaled).astype(BF16)
    rows_buf[...] = rows_all
    rows = rows_all[:rows_n]
    cot_rows = rows_all[rows_n:]

    part[:, used:] = jnp.zeros((n, full - used, LANES), F32)
    for load in loads[4:]:
        load.wait()
    for a, (left_arg, w_ref) in enumerate(
        ((rows, wg_ref), (rows, wu_ref), (cot_rows, wo_ref))
    ):
        product = nn(left_arg, w_ref[...])
        for r in range(rows_n // chunk):
            for c in range(lane_blocks):
                part[r * lane_blocks + c, a * chunk : (a + 1) * chunk] = product[
                    r * chunk : (r + 1) * chunk, c * LANES : (c + 1) * LANES
                ]

    def owner(step):
        return lax.rem(z + step + n, n)

    to_right = [STRIDE * (hops_right - s) for s in range(hops_right)]
    to_left = [-STRIDE * (hops_left - s) for s in range(hops_left)]
    order = []
    for s in range(hops_right):
        order += to_right[s : s + 1] + to_left[s : s + 1]
    order += [0]
    near_owners = {
        1: order,
        -1: order,
        2: [v - STRIDE for v in to_right],
        -2: to_left + [0],
    }
    near_base = {}
    total = 0
    for step, owners in near_owners.items():
        near_base[step] = total
        total += len(owners)

    def near_copy(step, k):
        at = near_base[step] + k
        return pltpu.make_async_remote_copy(
            src_ref=packed.at[at], dst_ref=near.at[at], send_sem=near_send.at[at],
            recv_sem=near_recv.at[at], device_id=along(step), device_id_type=MESH,
        )

    def send_near(targets):
        for target in targets:
            for step, owners in near_owners.items():
                if target in owners:
                    k = owners.index(target)
                    packed[near_base[step] + k] = part[owner(step + target)].astype(BF16)
                    near_copy(step, k).start()

    def targets_of(s):
        return to_right[s : s + 1] + to_left[s : s + 1] if s < hops_right else [0]

    def is_wide(way, s):
        return s >= (HALF_RIGHT if way > 0 else HALF_LEFT)

    def chain_copy(way, s, p):
        number = s if way > 0 else hops_right + s
        wide = is_wide(way, s)
        out, into = (full_out, full_in) if wide else (half_out, half_in)
        rows = pl.ds(p * piece, min(used, (p + 1) * piece) - p * piece if wide else piece)
        return pltpu.make_async_remote_copy(
            src_ref=out.at[number, rows], dst_ref=into.at[number, rows],
            send_sem=chain_send.at[number, p], recv_sem=chain_recv.at[number, p],
            device_id=along(way * STRIDE), device_id_type=MESH,
        )

    def arrived(way, s, p):
        number = s if way > 0 else hops_right + s
        chain_copy(way, s, p).wait_recv()
        return (full_in if is_wide(way, s) else half_in)[
            number, p * piece : (p + 1) * piece
        ].astype(F32)

    def around(target):
        value = part[owner(target)]
        for step, owners in near_owners.items():
            if target in owners:
                k = owners.index(target)
                near_copy(step, k).wait_recv()
                value = value + near[near_base[step] + k].astype(F32)
        return value

    def ways(s):
        return ((1, to_right), (-1, to_left)) if s < hops_left else ((1, to_right),)

    if used < full:
        full_in[:, used:] = jnp.zeros((leaders - 1, full - used, LANES), F32)
    send_near(targets_of(0))
    send_near(targets_of(1))
    for s in range(hops_right):
        here = {way: around(targets[s]) for way, targets in ways(s)}
        for p in range(PIECES):
            for way, _ in ways(s):
                value = here[way][p * piece : (p + 1) * piece]
                if s > 0:
                    value = value + arrived(way, s - 1, p)
                number = s if way > 0 else hops_right + s
                if is_wide(way, s):
                    full_out[number, p * piece : (p + 1) * piece] = value
                else:
                    half_out[number, p * piece : (p + 1) * piece] = value.astype(BF16)
                chain_copy(way, s, p).start()
        if s + 2 <= hops_right:
            send_near(targets_of(s + 2))
        if s == hops_left and hops_left:
            from_far_side = [arrived(-1, s - 1, p) for p in range(PIECES)]
    value = around(0)
    if hops_left:
        value = value + jnp.concatenate(from_far_side, axis=0)
    value = value + jnp.concatenate(
        [arrived(1, hops_right - 1, p) for p in range(PIECES)], axis=0
    )
    sums = [value[a * chunk : (a + 1) * chunk] for a in range(3)]

    gate_act, up_act, d_hidden = sums
    sig = jax.nn.sigmoid(gate_act)
    active = gate_act * sig
    grad_gate = d_hidden * up_act * (sig * (1.0 + gate_act * (1.0 - sig)))
    grad_up = d_hidden * active
    blank = [jnp.zeros((full - used, LANES), F32)] if used < full else []
    acts[z] = jnp.concatenate([active * up_act, grad_gate, grad_up] + blank, axis=0).astype(BF16)

    share_owners = {
        1: order,
        -1: order,
        2: [-STRIDE * k for k in range(hops_right)],
        -2: [STRIDE * k for k in range(hops_left + 1)],
    }

    def chain_back(way, s, held, p):
        number = s if way > 0 else hops_right + s
        place = acts.at[owner(held), pl.ds(p * piece, piece)]
        return pltpu.make_async_remote_copy(
            src_ref=place, dst_ref=place, send_sem=ag_send.at[number, p],
            recv_sem=ag_recv.at[number, p], device_id=along(way * STRIDE), device_id_type=MESH,
        )

    def share(step, held, k):
        at = near_base[step] + k
        place = acts.at[owner(held)]
        return pltpu.make_async_remote_copy(
            src_ref=place, dst_ref=place, send_sem=share_send.at[at],
            recv_sem=share_recv.at[at], device_id=along(step), device_id_type=MESH,
        )

    def unpack(held):
        place = owner(held)
        block = acts[place].astype(F32)
        row = pl.multiple_of((place // lane_blocks) * chunk, 8)
        col = pl.multiple_of(lax.rem(place, lane_blocks) * LANES, LANES)
        for a in range(3):
            wide_acts[a, pl.ds(row, chunk), pl.ds(col, LANES)] = block[
                a * chunk : (a + 1) * chunk
            ]

    def pass_on(held):
        for step, owners in share_owners.items():
            if held in owners:
                share(step, held, owners.index(held)).start()

    def taken(distance):
        for step, owners in share_owners.items():
            for k, held in enumerate(owners):
                if abs(held) == distance * STRIDE:
                    share(step, held - step, k).wait_recv()
                    unpack(held - step)

    for p in range(PIECES):
        for way, _ in ways(0):
            chain_back(way, 0, 0, p).start()
    pass_on(0)
    unpack(0)
    for s in range(1, hops_right + 1):
        coming = [(1, -STRIDE * s if s < hops_right else STRIDE * s)]
        if s <= hops_left:
            coming.append((-1, STRIDE * s))
        for p in range(PIECES):
            for way, held in coming:
                chain_back(way, s - 1, held, p).wait_recv()
                if s < (hops_right if way > 0 else hops_left):
                    chain_back(way, s, held, p).start()
        for _, held in coming:
            pass_on(held)
        for _, held in coming:
            unpack(held)
        taken(s - 1)
    taken(hops_right)

    hidden_all = wide_acts[0].astype(BF16)
    gg_all = wide_acts[1].astype(BF16)
    gu_all = wide_acts[2].astype(BF16)

    terms[:rows_n] = nt(hidden_all, wo_ref[...])
    terms[rows_n:] = nt(gg_all, wg_ref[...]) + nt(gu_all, wu_ref[...])
    whole = terms[...]
    high = whole.astype(BF16)
    low = (whole - high.astype(F32)).astype(BF16)
    table = select[...]
    per_token = nn(table, high) + nn(table, low)
    per_token = per_token * jnp.where(is_token, gate_mat[...], 1.0)
    outgo[...] = per_token.reshape(n, 2 * group, feats)

    def send_back(k):
        j = lax.rem(index + k, n)
        return pltpu.make_async_remote_copy(
            src_ref=outgo.at[j], dst_ref=income.at[index],
            send_sem=back_send.at[k], recv_sem=back_recv.at[index],
            device_id=peer(j), device_id_type=MESH,
        )

    def got_back(k):
        j = lax.rem(index + n - k, n)
        return pltpu.make_async_remote_copy(
            src_ref=outgo.at[j], dst_ref=income.at[j],
            send_sem=back_send.at[k], recv_sem=back_recv.at[j],
            device_id=peer(j), device_id_type=MESH,
        )

    lax.fori_loop(1, n, lambda k, _: (send_back(k).start(), 0)[1], 0)
    income[index] = outgo[index]

    rows_kept = rows_buf[:rows_n]
    do_ref[...] = tn(rows_buf[rows_n:], hidden_all).astype(BF16)
    dg_ref[...] = tn(rows_kept, gg_all).astype(BF16)
    du_ref[...] = tn(rows_kept, gu_all).astype(BF16)

    lax.fori_loop(1, n, lambda k, _: (got_back(k).wait_recv(), 0)[1], 0)
    last[...] = jnp.sum(income[...], axis=0).astype(BF16)

    def finish():
        return pltpu.make_async_remote_copy(
            src_ref=last, dst_ref=final, send_sem=end_sem.at[0],
            recv_sem=end_sem.at[1], device_id=partner, device_id_type=MESH,
        )

    @pl.when(away)
    def _():
        finish().start()

    @pl.when(jnp.logical_not(away))
    def _():
        final[...] = last[...]

    def sent_plane(k, _):
        spread(k).wait_send()
        send_back(k).wait_send()
        return 0

    lax.fori_loop(1, n, sent_plane, 0)

    for step, owners in near_owners.items():
        for k in range(len(owners)):
            near_copy(step, k).wait_send()
            share(step, 0, k).wait_send()
    for way, hops in ((1, hops_right), (-1, hops_left)):
        for s in range(hops):
            for p in range(PIECES):
                chain_copy(way, s, p).wait_send()
                chain_back(way, s, 0, p).wait_send()

    @pl.when(away)
    def _():
        finish().wait()

    done = final[...].astype(F32)
    mixed_ref[...] = done[:group].astype(BF16)
    dtok_ref[...] = done[group:].astype(BF16)


def per_device(n, tensor, experts, tokens, expert_ids, gates, w_gate, w_up, w_out, cotangent):
    group, model = tokens.shape
    _, hidden_units, feats = w_gate.shape
    capacity = 2 * (group // experts) + 1
    rows_n = capacity * n
    chunk = rows_n * (hidden_units // LANES) // n
    leaders = n // STRIDE
    hops = leaders - 1
    nears = 3 * leaders
    packed = -(-3 * chunk // (16 * PIECES)) * 16 * PIECES
    hbm = pl.BlockSpec(memory_space=pltpu.HBM)
    vmem = pl.BlockSpec(memory_space=pltpu.VMEM)
    dma = pltpu.SemaphoreType.DMA
    weight = jax.ShapeDtypeStruct((feats, hidden_units), BF16)
    small = jax.ShapeDtypeStruct((group, feats), BF16)
    mixed, d_tokens, d_gate, d_up, d_out = pl.pallas_call(
        functools.partial(kernel, (n, tensor, capacity)),
        out_shape=(small, small, weight, weight, weight),
        in_specs=[hbm] * 7,
        out_specs=(vmem,) * 5,
        scratch_shapes=[
            pltpu.VMEM(tokens.shape, BF16),
            pltpu.VMEM((2, group), jnp.int32),
            pltpu.VMEM((2, group), F32),
            pltpu.VMEM((feats, hidden_units), BF16),
            pltpu.VMEM((feats, hidden_units), BF16),
            pltpu.VMEM((feats, hidden_units), BF16),
            pltpu.VMEM(tokens.shape, BF16),
            dma((7,)),
            pltpu.VMEM((2 * group, 256), BF16),
            pltpu.VMEM((n, 2 * group, 256), BF16),
            pltpu.VMEM((n * 2 * group, 2 * rows_n), BF16),
            pltpu.VMEM((n * 2 * group, feats), F32),
            pltpu.VMEM((2 * rows_n, feats), BF16),
            pltpu.VMEM((n, packed, LANES), F32),
            pltpu.VMEM((nears, packed, LANES), BF16),
            pltpu.VMEM((nears, packed, LANES), BF16),
            pltpu.VMEM((hops, packed, LANES), BF16),
            pltpu.VMEM((hops, packed, LANES), BF16),
            pltpu.VMEM((hops, packed, LANES), F32),
            pltpu.VMEM((hops, packed, LANES), F32),
            pltpu.VMEM((n, packed, LANES), BF16),
            pltpu.VMEM((3, rows_n, hidden_units), F32),
            pltpu.VMEM((2 * rows_n, feats), F32),
            pltpu.VMEM((n, 2 * group, feats), F32),
            pltpu.VMEM((n, 2 * group, feats), F32),
            pltpu.VMEM((2 * group, feats), BF16),
            pltpu.VMEM((2 * group, feats), BF16),
            dma((2,)),
            dma((n,)),
            dma((n,)),
            dma((nears,)),
            dma((nears,)),
            dma((hops, PIECES)),
            dma((hops, PIECES)),
            dma((hops, PIECES)),
            dma((hops, PIECES)),
            dma((nears,)),
            dma((nears,)),
            dma((n,)),
            dma((n,)),
            dma((2,)),
        ],
        compiler_params=pltpu.CompilerParams(
            collective_id=0, has_side_effects=True, vmem_limit_bytes=40 * 1024 * 1024
        ),
    )(
        tokens, expert_ids.T, gates.T, w_gate[0].T, w_up[0].T, w_out[0].T, cotangent
    )
    return (mixed, d_tokens, d_gate.T[None], d_up.T[None], d_out.T[None])


def solution(mesh):
    sizes = (mesh.shape["dp"], mesh.shape["tensor"], mesh.shape["expert"])
    return jax.shard_map(
        functools.partial(per_device, *sizes),
        mesh=mesh,
        in_specs=(
            P("dp", None),
            P("dp", None),
            P("dp", None),
            P("expert", "tensor", "dp"),
            P("expert", "tensor", "dp"),
            P("expert", "tensor", "dp"),
            P("dp", None),
        ),
        out_specs=(
            P("dp", ("expert", "tensor")),
            P("dp", ("expert", "tensor")),
            P("expert", "tensor", "dp"),
            P("expert", "tensor", "dp"),
            P("expert", "tensor", "dp"),
        ),
        check_vma=False,
    )
```

```python
import functools

import jax
import jax.numpy as jnp
from jax import lax
from jax.experimental import pallas as pl
from jax.experimental.pallas import tpu as pltpu
from jax.sharding import PartitionSpec as P

MESH = pl.DeviceIdType.MESH
F32 = jnp.float32
BF16 = jnp.bfloat16
LANES = 128
EMPTY = -1024.0
STRIDE = 4
PIECES = 2
NEIGHBOURS = (1, -1, 2, -2, STRIDE, -STRIDE)
HALF_RIGHT = 2
HALF_LEFT = 1


def iota(shape, axis):
    return lax.broadcasted_iota(jnp.int32, shape, axis)


def nn(a, b):
    return jnp.dot(a, b, preferred_element_type=F32)


def nt(a, b):
    return lax.dot_general(a, b, (((1,), (1,)), ((), ())), preferred_element_type=F32)


def tn(a, b):
    return lax.dot_general(a, b, (((0,), (0,)), ((), ())), preferred_element_type=F32)


def split3(v):
    hi = v.astype(BF16).astype(F32)
    mid = (v - hi).astype(BF16).astype(F32)
    return hi, mid, v - hi - mid


def source_block(index, feats, tok_ref, cot_ref, ids_ref, gates_ref):
    group = tok_ref.shape[0]
    wide = 2 * feats

    def features(ref):
        start = pl.multiple_of((index // 2) * wide, LANES)
        pair = ref[:, pl.ds(start, wide)].astype(F32)
        turned = pltpu.roll(pair, feats, 1)
        odd = lax.rem(jnp.full((group, wide), index, jnp.int32), 2) == 1
        return jnp.where(odd, turned, pair)[:, :256]

    eye = iota((group, group), 0) == iota((group, group), 1)
    before = iota((group, group), 1) < iota((group, group), 0)

    def column(row):
        spread = jnp.broadcast_to(row, (group, group))
        return jnp.sum(jnp.where(eye, spread, 0.0), axis=1, keepdims=True)

    ids = ids_ref[...].astype(F32)
    id_rows = [ids[k : k + 1, :] for k in range(2)]
    id_cols = [column(row) for row in id_rows]
    gate_cols = [column(gates_ref[k : k + 1, :]) for k in range(2)]

    def slots(k):
        own = jnp.broadcast_to(id_cols[k], (group, group))
        same = [
            (own == jnp.broadcast_to(row, (group, group))).astype(F32) for row in id_rows
        ]
        return jnp.sum(jnp.where(before, same[0] + same[1], 0.0), axis=1, keepdims=True)

    lane = iota((group, 256), 1)

    def per_expert(offset, values, other):
        at = (lane - offset).astype(F32)
        return jnp.where(
            at == id_cols[0], values[0], jnp.where(at == id_cols[1], values[1], other)
        )

    parts = [split3(column) for column in gate_cols]
    meta = per_expert(feats, [slots(0), slots(1)], EMPTY)
    for n in range(3):
        gate = per_expert(feats + 8 * (n + 1), [parts[0][n], parts[1][n]], 0.0)
        meta = jnp.where(lane >= feats + 8 * (n + 1), gate, meta)

    def joined(ref):
        return jnp.where(lane < feats, features(ref), meta)

    return jnp.concatenate([joined(tok_ref), joined(cot_ref)], axis=0).astype(BF16)


def kernel(
    sizes,
    tok_hbm, ids_hbm, gates_hbm, wg_hbm, wu_hbm, wo_hbm, cot_hbm,
    mixed_ref, dtok_ref, dg_hbm, du_hbm, do_hbm,
    tok_ref, ids_ref, gates_ref, wg_ref, wu_ref, wo_ref, cot_ref, load_sem,
    dg_ref, du_ref, do_ref, store_sem, places, blk, gathered, select, gate_mat, rows_buf, part, packed, near, half_out, half_in, full_out, full_in,
    acts, wide_acts, terms, outgo, income, last, final,
    swap_sem, plane_send, plane_recv, near_send, near_recv, chain_send, chain_recv,
    ag_send, ag_recv, share_send, share_recv, back_send, back_recv, end_sem,
):
    n, tensor, capacity = sizes
    feats, hidden_units = wg_hbm.shape
    group = tok_ref.shape[0]
    rows_n = capacity * n
    leaders = n // STRIDE
    hops_right = leaders // 2
    hops_left = leaders - 1 - hops_right
    lane_blocks = hidden_units // LANES
    chunk = rows_n * lane_blocks // n
    used, full = 3 * chunk, part.shape[1]
    piece = full // PIECES

    loads = [
        pltpu.make_async_copy(src, dst, load_sem.at[k])
        for k, (src, dst) in enumerate((
            (tok_hbm, tok_ref), (cot_hbm, cot_ref), (ids_hbm, ids_ref), (gates_hbm, gates_ref),
            (wg_hbm, wg_ref), (wu_hbm, wu_ref), (wo_hbm, wo_ref),
        ))
    ]
    z = lax.axis_index("dp")
    e = lax.axis_index("expert")
    t = lax.axis_index("tensor")
    index = e * tensor + t

    def along(step):
        return (lax.rem(z + step + n, n), e, t)

    partner = (index, z // tensor, lax.rem(z, tensor))
    away = z != index

    def peer(j):
        return (z, j // tensor, lax.rem(j, tensor))

    barrier = pltpu.get_barrier_semaphore()

    @pl.when(away)
    def _():
        pl.semaphore_signal(barrier, inc=1, device_id=partner, device_id_type=MESH)

    for step in NEIGHBOURS:
        pl.semaphore_signal(barrier, inc=1, device_id=along(step), device_id_type=MESH)

    for load in loads:
        load.start()

    def greet(k, _):
        j = lax.rem(index + k, n)
        pl.semaphore_signal(barrier, inc=1, device_id=peer(j), device_id_type=MESH)
        return 0

    lax.fori_loop(1, n, greet, 0)
    for load in loads[:4]:
        load.wait()
    lines = n * 2 * group
    line = iota((lines, 2 * rows_n), 0)
    inner = lax.rem(line, 2 * group)
    place = capacity * (line // (2 * group)) + jnp.where(inner < group, 0, rows_n)
    places[...] = (place - iota((lines, 2 * rows_n), 1)).astype(F32)
    part[:, used:] = jnp.zeros((n, full - used, LANES), F32)
    full_in[:, used:] = jnp.zeros((leaders - 1, full - used, LANES), F32)
    blk[...] = source_block(index, feats, tok_ref, cot_ref, ids_ref, gates_ref)
    pl.semaphore_wait(barrier, n - 1 + len(NEIGHBOURS) + jnp.where(away, 1, 0))

    def swap():
        return pltpu.make_async_remote_copy(
            src_ref=blk, dst_ref=gathered.at[z], send_sem=swap_sem.at[0],
            recv_sem=swap_sem.at[1], device_id=partner, device_id_type=MESH,
        )

    @pl.when(away)
    def _():
        swap().start()
        swap().wait()

    @pl.when(jnp.logical_not(away))
    def _():
        gathered[index] = blk[...]

    def spread(k):
        j = lax.rem(index + k, n)
        return pltpu.make_async_remote_copy(
            src_ref=gathered.at[index], dst_ref=gathered.at[index],
            send_sem=plane_send.at[k], recv_sem=plane_recv.at[index],
            device_id=peer(j), device_id_type=MESH,
        )

    def arrival(k):
        j = lax.rem(index + n - k, n)
        return pltpu.make_async_remote_copy(
            src_ref=gathered.at[j], dst_ref=gathered.at[j],
            send_sem=plane_send.at[k], recv_sem=plane_recv.at[j],
            device_id=peer(j), device_id_type=MESH,
        )

    lax.fori_loop(1, n, lambda k, _: (spread(k).start(), 0)[1], 0)
    lax.fori_loop(1, n, lambda k, _: (arrival(k).wait_recv(), 0)[1], 0)

    block = gathered[...].reshape(lines, 256)
    meta = block[:, LANES:]
    base = feats - LANES
    pick = (iota((LANES, 2 * rows_n), 0) == base + e).astype(F32).astype(BF16)
    sel = (nn(meta, pick) + places[...] == 0.0).astype(F32)
    sel = sel.astype(BF16)
    select[...] = sel
    depth = iota((LANES, feats), 0) - base - e
    gate_pick = ((depth == 8) | (depth == 16) | (depth == 24)).astype(F32).astype(BF16)
    gate = nn(meta, gate_pick)
    gate_mat[...] = gate
    is_token = lax.rem(iota((lines, feats), 0), 2 * group) < group
    scaled = (block[:, :feats].astype(F32) * jnp.where(is_token, 1.0, gate)).astype(BF16)
    rows_all = tn(sel, scaled).astype(BF16)
    rows_buf[...] = rows_all
    rows = rows_all[:rows_n]
    cot_rows = rows_all[rows_n:]

    for load in loads[4:]:
        load.wait()
    for a, (left_arg, w_ref) in enumerate(
        ((rows, wg_ref), (rows, wu_ref), (cot_rows, wo_ref))
    ):
        product = nn(left_arg, w_ref[...])
        for r in range(rows_n // chunk):
            for c in range(lane_blocks):
                part[r * lane_blocks + c, a * chunk : (a + 1) * chunk] = product[
                    r * chunk : (r + 1) * chunk, c * LANES : (c + 1) * LANES
                ]

    def owner(step):
        return lax.rem(z + step + n, n)

    to_right = [STRIDE * (hops_right - s) for s in range(hops_right)]
    to_left = [-STRIDE * (hops_left - s) for s in range(hops_left)]
    order = []
    for s in range(hops_right):
        order += to_right[s : s + 1] + to_left[s : s + 1]
    order += [0]
    near_owners = {
        1: order,
        -1: order,
        2: [v - STRIDE for v in to_right],
        -2: to_left + [0],
    }
    near_base = {}
    total = 0
    for step, owners in near_owners.items():
        near_base[step] = total
        total += len(owners)

    def near_copy(step, k):
        at = near_base[step] + k
        return pltpu.make_async_remote_copy(
            src_ref=packed.at[at], dst_ref=near.at[at], send_sem=near_send.at[at],
            recv_sem=near_recv.at[at], device_id=along(step), device_id_type=MESH,
        )

    def send_near(targets):
        for target in targets:
            for step, owners in near_owners.items():
                if target in owners:
                    k = owners.index(target)
                    packed[near_base[step] + k] = part[owner(step + target)].astype(BF16)
                    near_copy(step, k).start()

    def targets_of(s):
        return to_right[s : s + 1] + to_left[s : s + 1] if s < hops_right else [0]

    def is_wide(way, s):
        return s >= (HALF_RIGHT if way > 0 else HALF_LEFT)

    def chain_copy(way, s, p):
        number = s if way > 0 else hops_right + s
        wide = is_wide(way, s)
        out, into = (full_out, full_in) if wide else (half_out, half_in)
        rows = pl.ds(p * piece, min(used, (p + 1) * piece) - p * piece if wide else piece)
        return pltpu.make_async_remote_copy(
            src_ref=out.at[number, rows], dst_ref=into.at[number, rows],
            send_sem=chain_send.at[number, p], recv_sem=chain_recv.at[number, p],
            device_id=along(way * STRIDE), device_id_type=MESH,
        )

    def arrived(way, s, p):
        number = s if way > 0 else hops_right + s
        chain_copy(way, s, p).wait_recv()
        return (full_in if is_wide(way, s) else half_in)[
            number, p * piece : (p + 1) * piece
        ].astype(F32)

    def around(target):
        value = part[owner(target)]
        for step, owners in near_owners.items():
            if target in owners:
                k = owners.index(target)
                near_copy(step, k).wait_recv()
                value = value + near[near_base[step] + k].astype(F32)
        return value

    def ways(s):
        return ((1, to_right), (-1, to_left)) if s < hops_left else ((1, to_right),)

    send_near(targets_of(0))
    send_near(targets_of(1))
    for s in range(hops_right):
        here = {way: around(targets[s]) for way, targets in ways(s)}
        for p in range(PIECES):
            for way, _ in ways(s):
                value = here[way][p * piece : (p + 1) * piece]
                if s > 0:
                    value = value + arrived(way, s - 1, p)
                number = s if way > 0 else hops_right + s
                if is_wide(way, s):
                    full_out[number, p * piece : (p + 1) * piece] = value
                else:
                    half_out[number, p * piece : (p + 1) * piece] = value.astype(BF16)
                chain_copy(way, s, p).start()
        if s + 2 <= hops_right:
            send_near(targets_of(s + 2))
        if s == hops_left and hops_left:
            from_far_side = [arrived(-1, s - 1, p) for p in range(PIECES)]
    value = around(0)
    if hops_left:
        value = value + jnp.concatenate(from_far_side, axis=0)
    value = value + jnp.concatenate(
        [arrived(1, hops_right - 1, p) for p in range(PIECES)], axis=0
    )
    sums = [value[a * chunk : (a + 1) * chunk] for a in range(3)]

    gate_act, up_act, d_hidden = sums
    sig = jax.nn.sigmoid(gate_act)
    active = gate_act * sig
    grad_gate = d_hidden * up_act * (sig * (1.0 + gate_act * (1.0 - sig)))
    grad_up = d_hidden * active
    blank = [jnp.zeros((full - used, LANES), F32)] if used < full else []
    acts[z] = jnp.concatenate([active * up_act, grad_gate, grad_up] + blank, axis=0).astype(BF16)

    share_owners = {
        1: order,
        -1: order,
        2: [-STRIDE * k for k in range(hops_right)],
        -2: [STRIDE * k for k in range(hops_left + 1)],
    }

    def chain_back(way, s, held, p):
        number = s if way > 0 else hops_right + s
        place = acts.at[owner(held), pl.ds(p * piece, piece)]
        return pltpu.make_async_remote_copy(
            src_ref=place, dst_ref=place, send_sem=ag_send.at[number, p],
            recv_sem=ag_recv.at[number, p], device_id=along(way * STRIDE), device_id_type=MESH,
        )

    def share(step, held, k):
        at = near_base[step] + k
        place = acts.at[owner(held)]
        return pltpu.make_async_remote_copy(
            src_ref=place, dst_ref=place, send_sem=share_send.at[at],
            recv_sem=share_recv.at[at], device_id=along(step), device_id_type=MESH,
        )

    def unpack(held):
        place = owner(held)
        block = acts[place].astype(F32)
        row = pl.multiple_of((place // lane_blocks) * chunk, 8)
        col = pl.multiple_of(lax.rem(place, lane_blocks) * LANES, LANES)
        for a in range(3):
            wide_acts[a, pl.ds(row, chunk), pl.ds(col, LANES)] = block[
                a * chunk : (a + 1) * chunk
            ]

    def pass_on(held):
        for step, owners in share_owners.items():
            if held in owners:
                share(step, held, owners.index(held)).start()

    def taken(distance):
        for step, owners in share_owners.items():
            for k, held in enumerate(owners):
                if abs(held) == distance * STRIDE:
                    share(step, held - step, k).wait_recv()
                    unpack(held - step)

    for p in range(PIECES):
        for way, _ in ways(0):
            chain_back(way, 0, 0, p).start()
    pass_on(0)
    unpack(0)
    for s in range(1, hops_right + 1):
        coming = [(1, -STRIDE * s if s < hops_right else STRIDE * s)]
        if s <= hops_left:
            coming.append((-1, STRIDE * s))
        for p in range(PIECES):
            for way, held in coming:
                chain_back(way, s - 1, held, p).wait_recv()
                if s < (hops_right if way > 0 else hops_left):
                    chain_back(way, s, held, p).start()
        for _, held in coming:
            pass_on(held)
        for _, held in coming:
            unpack(held)
        taken(s - 1)
    taken(hops_right)

    hidden_all = wide_acts[0].astype(BF16)
    gg_all = wide_acts[1].astype(BF16)
    gu_all = wide_acts[2].astype(BF16)

    terms[:rows_n] = nt(hidden_all, wo_ref[...])
    terms[rows_n:] = nt(gg_all, wg_ref[...]) + nt(gu_all, wu_ref[...])
    whole = terms[...]
    high = whole.astype(BF16)
    low = (whole - high.astype(F32)).astype(BF16)
    table = select[...]
    per_token = nn(table, high) + nn(table, low)
    per_token = per_token * jnp.where(is_token, gate_mat[...], 1.0)
    outgo[...] = per_token.reshape(n, 2 * group, feats)

    def send_back(k):
        j = lax.rem(index + k, n)
        return pltpu.make_async_remote_copy(
            src_ref=outgo.at[j], dst_ref=income.at[index],
            send_sem=back_send.at[k], recv_sem=back_recv.at[index],
            device_id=peer(j), device_id_type=MESH,
        )

    def got_back(k):
        j = lax.rem(index + n - k, n)
        return pltpu.make_async_remote_copy(
            src_ref=outgo.at[j], dst_ref=income.at[j],
            send_sem=back_send.at[k], recv_sem=back_recv.at[j],
            device_id=peer(j), device_id_type=MESH,
        )

    lax.fori_loop(1, n, lambda k, _: (send_back(k).start(), 0)[1], 0)
    income[index] = outgo[index]

    rows_kept = rows_buf[:rows_n]
    stores = []
    for k, (own, acts_all, buf, out) in enumerate((
        (rows_buf[rows_n:], hidden_all, do_ref, do_hbm),
        (rows_kept, gg_all, dg_ref, dg_hbm),
        (rows_kept, gu_all, du_ref, du_hbm),
    )):
        buf[...] = tn(own, acts_all).astype(BF16)
        stores.append(pltpu.make_async_copy(buf, out, store_sem.at[k]))
        stores[k].start()

    lax.fori_loop(1, n, lambda k, _: (got_back(k).wait_recv(), 0)[1], 0)
    last[...] = jnp.sum(income[...], axis=0).astype(BF16)

    def finish():
        return pltpu.make_async_remote_copy(
            src_ref=last, dst_ref=final, send_sem=end_sem.at[0],
            recv_sem=end_sem.at[1], device_id=partner, device_id_type=MESH,
        )

    @pl.when(away)
    def _():
        finish().start()

    @pl.when(jnp.logical_not(away))
    def _():
        final[...] = last[...]

    def sent_plane(k, _):
        spread(k).wait_send()
        send_back(k).wait_send()
        return 0

    lax.fori_loop(1, n, sent_plane, 0)

    for step, owners in near_owners.items():
        for k in range(len(owners)):
            near_copy(step, k).wait_send()
            share(step, 0, k).wait_send()
    for way, hops in ((1, hops_right), (-1, hops_left)):
        for s in range(hops):
            for p in range(PIECES):
                chain_copy(way, s, p).wait_send()
                chain_back(way, s, 0, p).wait_send()

    for store in stores:
        store.wait()

    @pl.when(away)
    def _():
        finish().wait()

    done = final[...].astype(F32)
    mixed_ref[...] = done[:group].astype(BF16)
    dtok_ref[...] = done[group:].astype(BF16)


def hand_out(*refs):
    count = len(refs) // 3
    taken, given, held = refs[:count], refs[count : 2 * count], refs[2 * count : 3 * count]
    in_sem, out_sem = refs[3 * count :]
    loads = [pltpu.make_async_copy(taken[k], held[k], in_sem.at[k]) for k in range(count)]
    stores = [pltpu.make_async_copy(held[k], given[k], out_sem.at[k]) for k in range(count)]
    for load in loads:
        load.start()
    for load, store in zip(loads, stores):
        load.wait()
        store.start()
    for store in stores:
        store.wait()


def per_device(n, tensor, experts, tokens, expert_ids, gates, w_gate, w_up, w_out, cotangent):
    group, model = tokens.shape
    _, hidden_units, feats = w_gate.shape
    capacity = 2 * (group // experts) + 1
    rows_n = capacity * n
    chunk = rows_n * (hidden_units // LANES) // n
    leaders = n // STRIDE
    hops = leaders - 1
    nears = 3 * leaders
    packed = -(-3 * chunk // (16 * PIECES)) * 16 * PIECES
    hbm = pl.BlockSpec(memory_space=pltpu.HBM)
    vmem = pl.BlockSpec(memory_space=pltpu.VMEM)
    dma = pltpu.SemaphoreType.DMA
    weight = jax.ShapeDtypeStruct((feats, hidden_units), BF16)
    small = jax.ShapeDtypeStruct((group, feats), BF16)
    shapes = (small, small, weight, weight, weight)
    results = pl.pallas_call(
        functools.partial(kernel, (n, tensor, capacity)),
        out_shape=shapes,
        in_specs=[hbm] * 7,
        out_specs=(vmem, vmem, hbm, hbm, hbm),
        scratch_shapes=[
            pltpu.VMEM(tokens.shape, BF16),
            pltpu.VMEM((2, group), jnp.int32),
            pltpu.VMEM((2, group), F32),
            pltpu.VMEM((feats, hidden_units), BF16),
            pltpu.VMEM((feats, hidden_units), BF16),
            pltpu.VMEM((feats, hidden_units), BF16),
            pltpu.VMEM(tokens.shape, BF16),
            dma((7,)),
            pltpu.VMEM((feats, hidden_units), BF16),
            pltpu.VMEM((feats, hidden_units), BF16),
            pltpu.VMEM((feats, hidden_units), BF16),
            dma((3,)),
            pltpu.VMEM((n * 2 * group, 2 * rows_n), F32),
            pltpu.VMEM((2 * group, 256), BF16),
            pltpu.VMEM((n, 2 * group, 256), BF16),
            pltpu.VMEM((n * 2 * group, 2 * rows_n), BF16),
            pltpu.VMEM((n * 2 * group, feats), F32),
            pltpu.VMEM((2 * rows_n, feats), BF16),
            pltpu.VMEM((n, packed, LANES), F32),
            pltpu.VMEM((nears, packed, LANES), BF16),
            pltpu.VMEM((nears, packed, LANES), BF16),
            pltpu.VMEM((hops, packed, LANES), BF16),
            pltpu.VMEM((hops, packed, LANES), BF16),
            pltpu.VMEM((hops, packed, LANES), F32),
            pltpu.VMEM((hops, packed, LANES), F32),
            pltpu.VMEM((n, packed, LANES), BF16),
            pltpu.VMEM((3, rows_n, hidden_units), F32),
            pltpu.VMEM((2 * rows_n, feats), F32),
            pltpu.VMEM((n, 2 * group, feats), F32),
            pltpu.VMEM((n, 2 * group, feats), F32),
            pltpu.VMEM((2 * group, feats), BF16),
            pltpu.VMEM((2 * group, feats), BF16),
            dma((2,)),
            dma((n,)),
            dma((n,)),
            dma((nears,)),
            dma((nears,)),
            dma((hops, PIECES)),
            dma((hops, PIECES)),
            dma((hops, PIECES)),
            dma((hops, PIECES)),
            dma((nears,)),
            dma((nears,)),
            dma((n,)),
            dma((n,)),
            dma((2,)),
        ],
        compiler_params=pltpu.CompilerParams(
            collective_id=0, has_side_effects=True, vmem_limit_bytes=60 * 1024 * 1024
        ),
    )(
        tokens, expert_ids.T, gates.T, w_gate[0].T, w_up[0].T, w_out[0].T, cotangent
    )
    mixed, d_tokens, d_gate, d_up, d_out = pl.pallas_call(
        hand_out,
        out_shape=shapes,
        in_specs=[hbm] * 5,
        out_specs=(hbm,) * 5,
        scratch_shapes=[pltpu.VMEM(v.shape, BF16) for v in shapes] + [dma((5,)), dma((5,))],
        compiler_params=pltpu.CompilerParams(vmem_limit_bytes=60 * 1024 * 1024),
    )(*results)
    return (mixed, d_tokens, d_gate.T[None], d_up.T[None], d_out.T[None])


def solution(mesh):
    sizes = (mesh.shape["dp"], mesh.shape["tensor"], mesh.shape["expert"])
    return jax.shard_map(
        functools.partial(per_device, *sizes),
        mesh=mesh,
        in_specs=(
            P("dp", None),
            P("dp", None),
            P("dp", None),
            P("expert", "tensor", "dp"),
            P("expert", "tensor", "dp"),
            P("expert", "tensor", "dp"),
            P("dp", None),
        ),
        out_specs=(
            P("dp", ("expert", "tensor")),
            P("dp", ("expert", "tensor")),
            P("expert", "tensor", "dp"),
            P("expert", "tensor", "dp"),
            P("expert", "tensor", "dp"),
        ),
        check_vma=False,
    )
```
